32 devices in a mesh: gx: 4 (over z), gy: 8 (over y, x, core).
Axes of the slice: x: 2, y: 2, z: 4, core: 2. Of those that a mesh axis runs over, the one named last changes fastest.
Arguments:
- a_blocks: float32 [256, 4, 128, 128], P(('gx', 'gy')), may hold values from -0.25 to 0.25
- a_cols: int32 [256, 4], replicated, may hold values from 0 to 255, as said below
- t_blocks: float32 [256, 128, 128], P(('gx', 'gy')), may hold values from -0.5 to 0.5
- t_agg: int32 [256], replicated, may hold values from 0 to 1, as said below
- dinv: float32 [256, 128, 128], P(('gx', 'gy')), may hold values from -0.5 to 0.5
- coarse_inv: float32 [64, 128, 128], P(('gx', 'gy')), may hold values from -1.5 to 1.5
Outputs:
- coarse: float32 [64, 14, 128, 128], P(('gx', 'gy'))
The draws below stay inside these ranges and needn't reach their ends.
Inputs may be any that keep to these rules, and one draw needn't show every extreme that they name: `a_cols`: block column 0 of row g is g itself; column 1 lies in g's own slab; column 2 lies in the slab below (on the cycle) and column 3 in the slab above; over the rows of one slab, columns 2 name exactly 4 distinct rows of the slab below, and columns 3 exactly 4 distinct rows of the slab above. `t_agg`: every slab's 2 aggregates each hold 4 of its rows.
All inputs are finite; a program needn't handle non-finite values.
Results may differ from the reference program's by a relative error of at most 0.0001.
Values sent between devices are 32-bit elements; how exact they have to be, the bound alone decides.
A program may use at most 64 MiB of HBM per device.

```python
import jax
import jax.numpy as jnp
from jax import lax

BLOCK = 128
SLOTS = 4
ROWS_DEV = 8
AGG_DEV = 2
FETCH = 4
COARSE_SLOTS = 14
FINE_ROWS = 256
AGGREGATES = 64


def row_orders(key, count):
    return jax.vmap(lambda subkey: jax.random.permutation(subkey, ROWS_DEV))(jax.random.split(key, count))


def build_graph(key):
    slab_count = FINE_ROWS // ROWS_DEV
    chosen = row_orders(jax.random.fold_in(key, 101), slab_count * 2)
    fetched = jnp.sort(chosen[:, :FETCH], axis=1).reshape(slab_count, 2, FETCH).astype(jnp.int32)
    ordering = row_orders(jax.random.fold_in(key, 202), slab_count * 2).reshape(slab_count, 2, ROWS_DEV)
    own_pick = jax.random.randint(jax.random.fold_in(key, 303), (slab_count, ROWS_DEV), 0, ROWS_DEV)
    slab_ids = jnp.arange(slab_count, dtype=jnp.int32)[:, None]
    row_ids = jnp.arange(ROWS_DEV, dtype=jnp.int32)[None, :]
    lower_slab = (slab_ids + slab_count - 1) % slab_count
    upper_slab = (slab_ids + 1) % slab_count
    pick_lower = jnp.take_along_axis(fetched[:, 0, :], ordering[:, 0, :] % FETCH, axis=1)
    pick_upper = jnp.take_along_axis(fetched[:, 1, :], ordering[:, 1, :] % FETCH, axis=1)
    columns = jnp.stack([slab_ids * ROWS_DEV + row_ids, slab_ids * ROWS_DEV + own_pick, lower_slab * ROWS_DEV + pick_lower, upper_slab * ROWS_DEV + pick_upper], axis=-1)
    return columns.reshape(FINE_ROWS, SLOTS).astype(jnp.int32)


def draw_a_cols(key, part):
    return build_graph(key)


def draw_t_agg(key, part):
    slab_count = FINE_ROWS // ROWS_DEV
    orders = row_orders(jax.random.fold_in(key, 404), slab_count)
    return (orders % AGG_DEV).reshape(FINE_ROWS).astype(jnp.int32)


def level_of(rng, dims, shards, least, top_value):
    def one(axis_at, parts):
        heights = jax.random.uniform(jax.random.fold_in(jax.random.fold_in(rng, 6), axis_at), (parts,), jnp.float32, least / len(shards), top_value / len(shards))
        return jnp.repeat(jnp.exp(heights), dims[axis_at] // parts).reshape((-1,) + (1,) * (len(dims) - axis_at - 1))

    gain = one(*shards[0])
    for cut in shards[1:]:
        gain = gain * one(*cut)
    return gain


def scatter_about(key, extent, deviation, bound, shards=(), kind=jnp.bfloat16):
    factor_of = level_of(key, extent, shards, -0.22, 0.18) if shards else 1.0
    values = jax.random.normal(key, extent, jnp.float32) * deviation * factor_of
    return jnp.minimum(jnp.maximum(values, -bound), bound).astype(kind)


def setup_inputs(seed: int = 0) -> dict:
    streams_of = jax.random.split(jax.random.key(seed), 7)
    return {
        "a_blocks": scatter_about(streams_of[0], (FINE_ROWS, SLOTS, BLOCK, BLOCK), (SLOTS * BLOCK) ** -0.5, 0.25, ((0, 32),), jnp.float32),
        "a_cols": draw_a_cols(jax.random.fold_in(streams_of[6], 71), 0),
        "t_blocks": scatter_about(streams_of[2], (FINE_ROWS, BLOCK, BLOCK), BLOCK ** -0.5, 0.5, ((0, 32),), jnp.float32),
        "t_agg": draw_t_agg(jax.random.fold_in(streams_of[6], 71), 0),
        "dinv": scatter_about(streams_of[4], (FINE_ROWS, BLOCK, BLOCK), BLOCK ** -0.5, 0.5, ((0, 32),), jnp.float32),
        "coarse_inv": scatter_about(streams_of[5], (AGGREGATES, BLOCK, BLOCK), 0.25, 1.5, ((0, 32),), jnp.float32),
    }


OMEGA = 0.6


def reference(a_blocks, a_cols, t_blocks, t_agg, dinv, coarse_inv):
    highest = lax.Precision.HIGHEST
    slab_count = FINE_ROWS // ROWS_DEV
    labels = (jnp.arange(FINE_ROWS, dtype=jnp.int32) // ROWS_DEV) * AGG_DEV + t_agg
    t_cols = t_blocks[a_cols]
    prod_at = jnp.einsum("gkab,gkbc->gkac", a_blocks, t_cols, precision=highest)
    smoothed = jnp.einsum("gab,gkbc->gkac", dinv, prod_at, precision=highest)
    first = (jnp.arange(SLOTS) == 0).astype(jnp.float32)
    prolong = first[None, :, None, None] * t_blocks[:, None] - OMEGA * smoothed
    near_labels = labels[a_cols]

    def accumulate(row, galerkin):
        columns = a_cols[row]
        gathered = prolong[columns]
        partial_value = jnp.einsum("kab,kqbc->kqac", a_blocks[row], gathered, precision=highest)
        contrib = jnp.einsum("pba,kqbc->pkqac", prolong[row], partial_value, precision=highest)
        near = near_labels[row]
        far = near_labels[columns]
        slot = ((far[None] // AGG_DEV - near[:, None, None] // AGG_DEV + 3) % slab_count) * AGG_DEV + far[None] % AGG_DEV
        target = jnp.broadcast_to(near[:, None, None], slot.shape)
        return galerkin.at[target.reshape(-1), slot.reshape(-1)].add(contrib.reshape(-1, BLOCK, BLOCK))

    galerkin = jnp.zeros((AGGREGATES, COARSE_SLOTS, BLOCK, BLOCK), jnp.float32)
    galerkin = lax.fori_loop(0, FINE_ROWS, accumulate, galerkin)
    return jnp.einsum("aij,asjk->asik", coarse_inv, galerkin, precision=highest)
```

```python
import functools

import jax
import jax.numpy as jnp
from jax import lax
from jax.experimental import pallas as pl
from jax.experimental.pallas import tpu as pltpu
from jax.sharding import PartitionSpec as P

AGG_DEV = 2

OMEGA = 0.6

F32 = jnp.float32
BF16 = jnp.bfloat16
MESH = pl.DeviceIdType.MESH

SEND_ORDER = (1, 3, 2, 0, 4)
FINAL_ORDER = (1, 5, 3, 2, 0, 4, 6)


def read_list(a_cols, slab, side, rows):
    block_cols = lax.dynamic_slice_in_dim(a_cols, slab * rows, rows, 0)[:, 2 + side]
    offsets = block_cols % rows
    counter = jnp.arange(rows, dtype=jnp.int32)
    is_read = jnp.any(offsets[:, None] == counter[None, :], axis=0).astype(jnp.int32)
    ranks = jnp.sum(jnp.where(counter[None, :] < counter[:, None], is_read[None, :], 0), axis=1)
    places = jnp.arange(rows // 2, dtype=jnp.int32)
    matched = (is_read[:, None] == 1) & (ranks[:, None] == places[None, :])
    return jnp.sum(jnp.where(matched, counter[:, None], 0), axis=0)


def indices(a_cols, t_agg, device, devices, rows):
    previous = (device + devices - 1) % devices
    following = (device + 1) % devices
    own = lax.dynamic_slice_in_dim(a_cols, device * rows, rows, 0)
    offsets = own % rows
    lower_list = read_list(a_cols, device, 0, rows)
    upper_list = read_list(a_cols, device, 1, rows)
    to_upper = read_list(a_cols, following, 0, rows)
    to_lower = read_list(a_cols, previous, 1, rows)
    places = jnp.arange(rows // 2, dtype=jnp.int32)

    def rank(entries, offs):
        return jnp.sum(jnp.where(entries[None, :] == offs[:, None], places[None, :], 0), axis=1)

    labels = t_agg[own]
    low_cols = a_cols[previous * rows + lower_list][:, 2:4]
    up_cols = a_cols[following * rows + upper_list][:, 2:4]
    low_labels = t_agg[low_cols]
    up_labels = t_agg[up_cols]
    return jnp.concatenate(
        [
            offsets[:, 1],
            rank(lower_list, offsets[:, 2]),
            rank(upper_list, offsets[:, 3]),
            labels.T.reshape(-1),
            to_upper,
            to_lower,
            low_labels.T.reshape(-1),
            up_labels.T.reshape(-1),
        ]
    ).astype(jnp.int32)


def split(x):
    high = x.astype(BF16)
    return high, (x - high.astype(F32)).astype(BF16)


def dot3(ah, al, bh, bl):
    def dot(x, y):
        return jnp.dot(x, y, preferred_element_type=F32)

    return dot(ah, bh) + (dot(ah, bl) + dot(al, bh))


def kernel(
    rows, gx_size, gy_size,
    idx, a_hbm, t_hbm, d_hbm, c_hbm, out,
    a_v, t_v, d_v, c_v,
    ah, al, bh, bl, th, tl,
    t_send, t_recv, own_c, far_c, po_send, po_recv, pf_send, pf_recv,
    pdh, pdl, ndh, ndl, pth, ptl, aph, apl,
    g_send, g_recv, g_own,
    load_sem, send_sem, recv_sem,
):
    fetch = rows // 2
    blk = t_v.shape[-1]
    wide = AGG_DEV * blk
    devices = gx_size * gy_size
    me = lax.axis_index("gx") * gy_size + lax.axis_index("gy")
    following = lax.rem(me + 1, devices)
    previous = lax.rem(me + devices - 1, devices)

    def place(d):
        return (d // gy_size, lax.rem(d, gy_size))

    targets = (place(following), place(previous))

    barrier = pltpu.get_barrier_semaphore()
    for target in targets:
        pl.semaphore_signal(barrier, inc=1, device_id=target, device_id_type=MESH)

    loads = []
    for n, (src, dst) in enumerate(((t_hbm, t_v), (d_hbm, d_v), (a_hbm, a_v), (c_hbm, c_v))):
        copy = pltpu.make_async_copy(src, dst, load_sem.at[n])
        copy.start()
        loads.append(copy)

    def send(src, dst, side, n):
        copy = pltpu.make_async_remote_copy(
            src_ref=src,
            dst_ref=dst,
            send_sem=send_sem.at[side, n],
            recv_sem=recv_sem.at[side, n],
            device_id=targets[side],
            device_id_type=MESH,
        )
        copy.start()
        return copy

    base_c1, base_lp, base_up = 0, rows, 2 * rows
    base_lab = 3 * rows
    base_to = 7 * rows
    base_near = base_to + 2 * fetch

    loads[0].wait()
    for side in range(2):
        for j in range(fetch):
            t_send[side, j] = t_v[idx[base_to + side * fetch + j]]
    pl.semaphore_wait(barrier, 2)
    t_copies = [send(t_send.at[side], t_recv.at[side], side, 0) for side in range(2)]

    loads[1].wait()
    loads[2].wait()

    @pl.loop(0, rows)
    def _(g):
        h, l = split(t_v[g])
        th[g], tl[g] = h, l
        dh, dl = split(d_v[g])
        for k in range(4):
            h, l = split(a_v[g, k])
            ah[g, :, k * blk:(k + 1) * blk] = h
            al[g, :, k * blk:(k + 1) * blk] = l
        h, l = split(-OMEGA * dot3(dh, dl, ah[g], al[g]))
        bh[g], bl[g] = h, l

    def mask(position, value):
        return (idx[position] == value).astype(F32)

    @pl.loop(0, rows)
    def _(g):
        c1 = idx[base_c1 + g]
        p0 = t_v[g] + dot3(bh[g, :, 0:blk], bl[g, :, 0:blk], th[g], tl[g])
        p1 = dot3(bh[g, :, blk:2 * blk], bl[g, :, blk:2 * blk], th[c1], tl[c1])
        for v in range(AGG_DEV):
            own_c[g, :, v * blk:(v + 1) * blk] = p0 * mask(base_lab + g, v) + p1 * mask(base_lab + rows + g, v)

    for side in range(2):
        for j in range(fetch):
            po_send[side, j] = own_c[idx[base_to + side * fetch + j]]
    po_copies = [send(po_send.at[side], po_recv.at[side], side, 1) for side in range(2)]

    for copy in t_copies:
        copy.wait_recv()

    for side in range(2):
        for j in range(fetch):
            h, l = split(t_recv[side, j])
            th[rows + side * fetch + j] = h
            tl[rows + side * fetch + j] = l

    @pl.loop(0, rows)
    def _(g):
        for side in range(2):
            at = rows + side * fetch + idx[(base_lp, base_up)[side] + g]
            cols = slice((2 + side) * blk, (3 + side) * blk)
            far_c[g, :, side * blk:(side + 1) * blk] = dot3(bh[g, :, cols], bl[g, :, cols], th[at], tl[at])

    for side in range(2):
        for j in range(fetch):
            pf_send[side, j] = far_c[idx[base_to + side * fetch + j]]
    pf_copies = [send(pf_send.at[side], pf_recv.at[side], side, 2) for side in range(2)]

    @pl.loop(0, rows)
    def _(g):
        at = pl.ds(pl.multiple_of(g * blk, blk), blk)
        h, l = split(own_c[g])
        pdh[g, 1], pdl[g, 1] = h, l
        for v in range(AGG_DEV):
            cols = slice(v * blk, (v + 1) * blk)
            h, l = split(own_c[g, :, cols].T)
            pth[1, cols, at] = h
            ptl[1, cols, at] = l
        for side in range(2):
            block = far_c[g, :, side * blk:(side + 1) * blk]
            flip = block.T
            for v in range(AGG_DEV):
                cols = slice(v * blk, (v + 1) * blk)
                keep = mask(base_lab + (2 + side) * rows + g, v)
                h, l = split(block * keep)
                pdh[g, 2 * side, :, cols] = h
                pdl[g, 2 * side, :, cols] = l
                h, l = split(flip * keep)
                pth[2 * side, cols, at] = h
                ptl[2 * side, cols, at] = l

    for copy in po_copies:
        copy.wait_recv()
    for side in range(2):
        for j in range(fetch):
            h, l = split(po_recv[side, j])
            ndh[side * fetch + j, 1] = h
            ndl[side * fetch + j, 1] = l

    def product(n):
        @pl.loop(0, rows)
        def _(g):
            c1 = idx[base_c1 + g]
            lp = idx[base_lp + g]
            up = fetch + idx[base_up + g]
            tops, bottoms = [], []
            parts = []
            if 1 <= n <= 3:
                parts += [(0, pdh, pdl, g, n - 1), (1, pdh, pdl, c1, n - 1)]
            if n <= 2:
                parts += [(2, ndh, ndl, lp, n)]
            if n >= 2:
                parts += [(3, ndh, ndl, up, n - 2)]
            for _, high, low, row, at in parts:
                tops.append(high[row, at])
                bottoms.append(low[row, at])
            slots = [p[0] for p in parts]
            if slots == list(range(slots[0], slots[0] + len(slots))):
                xh = ah[g, :, slots[0] * blk:(slots[-1] + 1) * blk]
                xl = al[g, :, slots[0] * blk:(slots[-1] + 1) * blk]
            else:
                xh = jnp.concatenate([ah[g, :, k * blk:(k + 1) * blk] for k in slots], axis=1)
                xl = jnp.concatenate([al[g, :, k * blk:(k + 1) * blk] for k in slots], axis=1)
            yh = jnp.concatenate(tops, axis=0) if len(tops) > 1 else tops[0]
            yl = jnp.concatenate(bottoms, axis=0) if len(bottoms) > 1 else bottoms[0]
            h, l = split(dot3(xh, xl, yh, yl))
            at = pl.ds(pl.multiple_of(g * blk, blk), blk)
            aph[n, at, :] = h
            apl[n, at, :] = l

    g_copies = {}

    def neighbours(n):
        for side in range(2):
            r = 2 - 2 * side
            g_send[side, n] = dot3(pth[r], ptl[r], aph[n], apl[n])
            g_copies[side, n] = send(g_send.at[side, n], g_recv.at[side, n], side, 3 + n)

    for n in SEND_ORDER[:2]:
        product(n)
        neighbours(n)

    for copy in pf_copies:
        copy.wait_recv()

    @pl.loop(0, fetch)
    def _(j):
        for owner in range(2):
            for side in range(2):
                block = pf_recv[owner, j, :, side * blk:(side + 1) * blk]
                for v in range(AGG_DEV):
                    keep = mask(base_near + (owner * 2 + side) * fetch + j, v)
                    h, l = split(block * keep)
                    cols = slice(v * blk, (v + 1) * blk)
                    ndh[owner * fetch + j, 2 * side, :, cols] = h
                    ndl[owner * fetch + j, 2 * side, :, cols] = l

    for n in SEND_ORDER[2:]:
        product(n)
        neighbours(n)

    for n in SEND_ORDER:
        g_own[n] = dot3(pth[1], ptl[1], aph[n], apl[n])

    loads[3].wait()
    inverses = [split(c_v[a]) for a in range(AGG_DEV)]
    for j in FINAL_ORDER:
        if j <= 4:
            g_copies[0, j].wait_recv()
        if j >= 2:
            g_copies[1, j - 2].wait_recv()
        for a in range(AGG_DEV):
            at = slice(a * blk, (a + 1) * blk)
            terms = []
            if 1 <= j <= 5:
                terms.append(g_own[j - 1, at, :])
            if j <= 4:
                terms.append(g_recv[0, j, at, :])
            if j >= 2:
                terms.append(g_recv[1, j - 2, at, :])
            h, l = split(functools.reduce(jnp.add, terms))
            result = dot3(inverses[a][0], inverses[a][1], h, l)
            for v in range(AGG_DEV):
                out[a, AGG_DEV * j + v] = result[:, v * blk:(v + 1) * blk]

    for copy in [*t_copies, *po_copies, *pf_copies, *g_copies.values()]:
        copy.wait_send()


def shards(gx_size, gy_size, a_blocks, a_cols, t_blocks, t_agg, dinv, coarse_inv):
    devices = gx_size * gy_size
    device = lax.axis_index(("gx", "gy"))
    rows, blk = t_blocks.shape[0], t_blocks.shape[1]
    fetch = rows // 2
    wide = AGG_DEV * blk
    idx = indices(a_cols, t_agg, device, devices, rows)
    hbm = pl.BlockSpec(memory_space=pl.ANY)
    scratch = [
        pltpu.VMEM(a_blocks.shape, F32),
        pltpu.VMEM(t_blocks.shape, F32),
        pltpu.VMEM(dinv.shape, F32),
        pltpu.VMEM(coarse_inv.shape, F32),
        *[pltpu.VMEM((rows, blk, 4 * blk), BF16)] * 4,
        *[pltpu.VMEM((rows + 2 * fetch, blk, blk), BF16)] * 2,
        *[pltpu.VMEM((2, fetch, blk, blk), F32)] * 2,
        *[pltpu.VMEM((rows, blk, wide), F32)] * 2,
        *[pltpu.VMEM((2, fetch, blk, wide), F32)] * 4,
        *[pltpu.VMEM((rows, 3, blk, wide), BF16)] * 2,
        *[pltpu.VMEM((2 * fetch, 3, blk, wide), BF16)] * 2,
        *[pltpu.VMEM((3, wide, rows * blk), BF16)] * 2,
        *[pltpu.VMEM((5, rows * blk, wide), BF16)] * 2,
        *[pltpu.VMEM((2, 5, wide, wide), F32)] * 2,
        pltpu.VMEM((5, wide, wide), F32),
        pltpu.SemaphoreType.DMA((4,)),
        pltpu.SemaphoreType.DMA((2, 8)),
        pltpu.SemaphoreType.DMA((2, 8)),
    ]
    return pl.pallas_call(
        functools.partial(kernel, rows, gx_size, gy_size),
        out_shape=jax.ShapeDtypeStruct((coarse_inv.shape[0], 7 * AGG_DEV, blk, blk), F32),
        in_specs=[pl.BlockSpec(memory_space=pltpu.SMEM), hbm, hbm, hbm, hbm],
        out_specs=pl.BlockSpec(memory_space=pltpu.VMEM),
        scratch_shapes=scratch,
        compiler_params=pltpu.CompilerParams(
            collective_id=0, has_side_effects=True, vmem_limit_bytes=56 * 1024 * 1024
        ),
    )(idx, a_blocks, t_blocks, dinv, coarse_inv)


def solution(mesh):
    placed = (
        P(("gx", "gy"), None, None, None),
        P(),
        P(("gx", "gy"), None, None),
        P(),
        P(("gx", "gy"), None, None),
        P(("gx", "gy"), None, None),
    )
    return jax.shard_map(
        functools.partial(shards, mesh.shape["gx"], mesh.shape["gy"]),
        mesh=mesh,
        in_specs=placed,
        out_specs=P(("gx", "gy"), None, None, None),
        check_vma=False,
    )
```

```python
import functools

import jax
import jax.numpy as jnp
from jax import lax
from jax.experimental import pallas as pl
from jax.experimental.pallas import tpu as pltpu
from jax.sharding import PartitionSpec as P

AGG_DEV = 2

OMEGA = 0.6

F32 = jnp.float32
BF16 = jnp.bfloat16
MESH = pl.DeviceIdType.MESH

SEND_ORDER = (1, 3, 2, 0, 4)
FINAL_ORDER = (1, 5, 3, 2, 0, 4, 6)


def read_lists(cols, labels, idx, rows, me, following, previous):
    fetch = rows // 2

    def offset(slab, row, k):
        return lax.rem(cols[(slab * rows + row) * 4 + k], rows)

    def one(value):
        return value.astype(jnp.int32)

    def read_list(slab, side):
        offs = [offset(slab, r, 2 + side) for r in range(rows)]
        read = [functools.reduce(jnp.maximum, [one(o == c) for o in offs]) for c in range(rows)]
        picks = [0] * fetch
        before = 0
        for c in range(rows):
            for j in range(max(0, c - fetch), min(c, fetch - 1) + 1):
                picks[j] = picks[j] + jnp.where(before == j, c * read[c], 0)
            before = before + read[c]
        return offs, read, picks

    base_to = 7 * rows
    for side, slab in ((0, following), (1, previous)):
        picks = read_list(slab, side)[2]
        for j in range(fetch):
            idx[base_to + side * fetch + j] = picks[j]

    def rest():
        for side, slab in ((0, previous), (1, following)):
            offs, read, picks = read_list(me, side)
            ranks = [0]
            for c in range(rows - 1):
                ranks.append(ranks[-1] + read[c])
            for r in range(rows):
                idx[(1 + side) * rows + r] = functools.reduce(
                    jnp.add, [jnp.where(offs[r] == c, ranks[c], 0) for c in range(1, rows)]
                )
            for j in range(fetch):
                for far in range(2):
                    entry = cols[(slab * rows + picks[j]) * 4 + 2 + far]
                    idx[base_to + 2 * fetch + (side * 2 + far) * fetch + j] = labels[entry]
        for r in range(rows):
            idx[r] = offset(me, r, 1)
            for k in range(4):
                idx[(3 + k) * rows + r] = labels[cols[(me * rows + r) * 4 + k]]

    return rest


def split(x):
    high = x.astype(BF16)
    return high, (x - high.astype(F32)).astype(BF16)


def dot3(ah, al, bh, bl):
    def dot(x, y):
        return jnp.dot(x, y, preferred_element_type=F32)

    return dot(ah, bh) + (dot(ah, bl) + dot(al, bh))


def kernel(
    rows, gx_size, gy_size,
    cols_s, labels_s, a_hbm, t_hbm, d_hbm, c_hbm, out,
    idx, out_v,
    a_v, t_v, d_v, c_v,
    ah, al, bh, bl, th, tl,
    t_send, t_recv, own_c, far_c, po_send, po_recv, pf_send, pf_recv,
    pdh, pdl, ndh, ndl, pth, ptl, aph, apl,
    g_send, g_recv, g_own,
    load_sem, send_sem, recv_sem, out_sem,
):
    fetch = rows // 2
    blk = t_v.shape[-1]
    wide = AGG_DEV * blk
    devices = gx_size * gy_size
    me = lax.axis_index("gx") * gy_size + lax.axis_index("gy")
    following = lax.rem(me + 1, devices)
    previous = lax.rem(me + devices - 1, devices)

    def place(d):
        return (d // gy_size, lax.rem(d, gy_size))

    targets = (place(following), place(previous))

    barrier = pltpu.get_barrier_semaphore()
    for target in targets:
        pl.semaphore_signal(barrier, inc=1, device_id=target, device_id_type=MESH)

    loads = []
    for n, (src, dst) in enumerate(((t_hbm, t_v), (d_hbm, d_v), (a_hbm, a_v), (c_hbm, c_v))):
        copy = pltpu.make_async_copy(src, dst, load_sem.at[n])
        copy.start()
        loads.append(copy)

    def send(src, dst, side, n):
        copy = pltpu.make_async_remote_copy(
            src_ref=src,
            dst_ref=dst,
            send_sem=send_sem.at[side, n],
            recv_sem=recv_sem.at[side, n],
            device_id=targets[side],
            device_id_type=MESH,
        )
        copy.start()
        return copy

    base_c1, base_lp, base_up = 0, rows, 2 * rows
    base_lab = 3 * rows
    base_to = 7 * rows
    base_near = base_to + 2 * fetch

    rest = read_lists(cols_s, labels_s, idx, rows, me, following, previous)
    loads[0].wait()
    for side in range(2):
        for j in range(fetch):
            t_send[side, j] = t_v[idx[base_to + side * fetch + j]]
    pl.semaphore_wait(barrier, 2)
    t_copies = [send(t_send.at[side], t_recv.at[side], side, 0) for side in range(2)]

    rest()
    loads[1].wait()
    loads[2].wait()

    @pl.loop(0, rows)
    def _(g):
        h, l = split(t_v[g])
        th[g], tl[g] = h, l
        dh, dl = split(d_v[g])
        for k in range(4):
            h, l = split(a_v[g, k])
            ah[g, :, k * blk:(k + 1) * blk] = h
            al[g, :, k * blk:(k + 1) * blk] = l
        h, l = split(-OMEGA * dot3(dh, dl, ah[g], al[g]))
        bh[g], bl[g] = h, l

    def mask(position, value):
        return (idx[position] == value).astype(F32)

    @pl.loop(0, rows)
    def _(g):
        c1 = idx[base_c1 + g]
        p0 = t_v[g] + dot3(bh[g, :, 0:blk], bl[g, :, 0:blk], th[g], tl[g])
        p1 = dot3(bh[g, :, blk:2 * blk], bl[g, :, blk:2 * blk], th[c1], tl[c1])
        for v in range(AGG_DEV):
            own_c[g, :, v * blk:(v + 1) * blk] = p0 * mask(base_lab + g, v) + p1 * mask(base_lab + rows + g, v)

    for side in range(2):
        for j in range(fetch):
            po_send[side, j] = own_c[idx[base_to + side * fetch + j]]
    po_copies = [send(po_send.at[side], po_recv.at[side], side, 1) for side in range(2)]

    for copy in t_copies:
        copy.wait_recv()

    for side in range(2):
        for j in range(fetch):
            h, l = split(t_recv[side, j])
            th[rows + side * fetch + j] = h
            tl[rows + side * fetch + j] = l

    @pl.loop(0, rows)
    def _(g):
        for side in range(2):
            at = rows + side * fetch + idx[(base_lp, base_up)[side] + g]
            cols = slice((2 + side) * blk, (3 + side) * blk)
            far_c[g, :, side * blk:(side + 1) * blk] = dot3(bh[g, :, cols], bl[g, :, cols], th[at], tl[at])

    for side in range(2):
        for j in range(fetch):
            pf_send[side, j] = far_c[idx[base_to + side * fetch + j]]
    pf_copies = [send(pf_send.at[side], pf_recv.at[side], side, 2) for side in range(2)]

    @pl.loop(0, rows)
    def _(g):
        at = pl.ds(pl.multiple_of(g * blk, blk), blk)
        h, l = split(own_c[g])
        pdh[g, 1], pdl[g, 1] = h, l
        for v in range(AGG_DEV):
            cols = slice(v * blk, (v + 1) * blk)
            h, l = split(own_c[g, :, cols].T)
            pth[1, cols, at] = h
            ptl[1, cols, at] = l
        for side in range(2):
            block = far_c[g, :, side * blk:(side + 1) * blk]
            flip = block.T
            for v in range(AGG_DEV):
                cols = slice(v * blk, (v + 1) * blk)
                keep = mask(base_lab + (2 + side) * rows + g, v)
                h, l = split(block * keep)
                pdh[g, 2 * side, :, cols] = h
                pdl[g, 2 * side, :, cols] = l
                h, l = split(flip * keep)
                pth[2 * side, cols, at] = h
                ptl[2 * side, cols, at] = l

    for copy in po_copies:
        copy.wait_recv()
    for side in range(2):
        for j in range(fetch):
            h, l = split(po_recv[side, j])
            ndh[side * fetch + j, 1] = h
            ndl[side * fetch + j, 1] = l

    def product(n):
        @pl.loop(0, rows)
        def _(g):
            c1 = idx[base_c1 + g]
            lp = idx[base_lp + g]
            up = fetch + idx[base_up + g]
            tops, bottoms = [], []
            parts = []
            if 1 <= n <= 3:
                parts += [(0, pdh, pdl, g, n - 1), (1, pdh, pdl, c1, n - 1)]
            if n <= 2:
                parts += [(2, ndh, ndl, lp, n)]
            if n >= 2:
                parts += [(3, ndh, ndl, up, n - 2)]
            for _, high, low, row, at in parts:
                tops.append(high[row, at])
                bottoms.append(low[row, at])
            slots = [p[0] for p in parts]
            if slots == list(range(slots[0], slots[0] + len(slots))):
                xh = ah[g, :, slots[0] * blk:(slots[-1] + 1) * blk]
                xl = al[g, :, slots[0] * blk:(slots[-1] + 1) * blk]
            else:
                xh = jnp.concatenate([ah[g, :, k * blk:(k + 1) * blk] for k in slots], axis=1)
                xl = jnp.concatenate([al[g, :, k * blk:(k + 1) * blk] for k in slots], axis=1)
            yh = jnp.concatenate(tops, axis=0) if len(tops) > 1 else tops[0]
            yl = jnp.concatenate(bottoms, axis=0) if len(bottoms) > 1 else bottoms[0]
            h, l = split(dot3(xh, xl, yh, yl))
            at = pl.ds(pl.multiple_of(g * blk, blk), blk)
            aph[n, at, :] = h
            apl[n, at, :] = l

    g_copies = {}

    def neighbours(n):
        for side in range(2):
            r = 2 - 2 * side
            g_send[side, n] = dot3(pth[r], ptl[r], aph[n], apl[n])
            g_copies[side, n] = send(g_send.at[side, n], g_recv.at[side, n], side, 3 + n)

    for n in SEND_ORDER[:2]:
        product(n)
        neighbours(n)

    for copy in pf_copies:
        copy.wait_recv()

    @pl.loop(0, fetch)
    def _(j):
        for owner in range(2):
            for side in range(2):
                block = pf_recv[owner, j, :, side * blk:(side + 1) * blk]
                for v in range(AGG_DEV):
                    keep = mask(base_near + (owner * 2 + side) * fetch + j, v)
                    h, l = split(block * keep)
                    cols = slice(v * blk, (v + 1) * blk)
                    ndh[owner * fetch + j, 2 * side, :, cols] = h
                    ndl[owner * fetch + j, 2 * side, :, cols] = l

    for n in SEND_ORDER[2:]:
        product(n)
        neighbours(n)

    for n in SEND_ORDER:
        g_own[n] = dot3(pth[1], ptl[1], aph[n], apl[n])

    loads[3].wait()
    inverses = [split(c_v[a]) for a in range(AGG_DEV)]
    stores = []
    for j in FINAL_ORDER:
        if j <= 4:
            g_copies[0, j].wait_recv()
        if j >= 2:
            g_copies[1, j - 2].wait_recv()
        for a in range(AGG_DEV):
            at = slice(a * blk, (a + 1) * blk)
            terms = []
            if 1 <= j <= 5:
                terms.append(g_own[j - 1, at, :])
            if j <= 4:
                terms.append(g_recv[0, j, at, :])
            if j >= 2:
                terms.append(g_recv[1, j - 2, at, :])
            h, l = split(functools.reduce(jnp.add, terms))
            result = dot3(inverses[a][0], inverses[a][1], h, l)
            for v in range(AGG_DEV):
                out_v[a, AGG_DEV * j + v] = result[:, v * blk:(v + 1) * blk]
            slots = pl.ds(AGG_DEV * j, AGG_DEV)
            store = pltpu.make_async_copy(out_v.at[a, slots], out.at[a, slots], out_sem.at[a, j])
            store.start()
            stores.append(store)

    for copy in [*t_copies, *po_copies, *pf_copies, *g_copies.values()]:
        copy.wait_send()
    for store in stores:
        store.wait()


def shards(gx_size, gy_size, a_blocks, a_cols, t_blocks, t_agg, dinv, coarse_inv):
    rows, blk = t_blocks.shape[0], t_blocks.shape[1]
    fetch = rows // 2
    wide = AGG_DEV * blk
    shape = (coarse_inv.shape[0], 7 * AGG_DEV, blk, blk)
    hbm = pl.BlockSpec(memory_space=pl.ANY)
    smem = pl.BlockSpec(memory_space=pltpu.SMEM)
    scratch = [
        pltpu.SMEM((7 * rows + 6 * fetch,), jnp.int32),
        pltpu.VMEM(shape, F32),
        pltpu.VMEM(a_blocks.shape, F32),
        pltpu.VMEM(t_blocks.shape, F32),
        pltpu.VMEM(dinv.shape, F32),
        pltpu.VMEM(coarse_inv.shape, F32),
        *[pltpu.VMEM((rows, blk, 4 * blk), BF16)] * 4,
        *[pltpu.VMEM((rows + 2 * fetch, blk, blk), BF16)] * 2,
        *[pltpu.VMEM((2, fetch, blk, blk), F32)] * 2,
        *[pltpu.VMEM((rows, blk, wide), F32)] * 2,
        *[pltpu.VMEM((2, fetch, blk, wide), F32)] * 4,
        *[pltpu.VMEM((rows, 3, blk, wide), BF16)] * 2,
        *[pltpu.VMEM((2 * fetch, 3, blk, wide), BF16)] * 2,
        *[pltpu.VMEM((3, wide, rows * blk), BF16)] * 2,
        *[pltpu.VMEM((5, rows * blk, wide), BF16)] * 2,
        *[pltpu.VMEM((2, 5, wide, wide), F32)] * 2,
        pltpu.VMEM((5, wide, wide), F32),
        pltpu.SemaphoreType.DMA((4,)),
        pltpu.SemaphoreType.DMA((2, 8)),
        pltpu.SemaphoreType.DMA((2, 8)),
        pltpu.SemaphoreType.DMA((AGG_DEV, 7)),
    ]
    return pl.pallas_call(
        functools.partial(kernel, rows, gx_size, gy_size),
        out_shape=jax.ShapeDtypeStruct(shape, F32),
        in_specs=[smem, smem, hbm, hbm, hbm, hbm],
        out_specs=hbm,
        scratch_shapes=scratch,
        compiler_params=pltpu.CompilerParams(
            collective_id=0, has_side_effects=True, vmem_limit_bytes=56 * 1024 * 1024
        ),
    )(a_cols.reshape(-1), t_agg, a_blocks, t_blocks, dinv, coarse_inv)


def solution(mesh):
    placed = (
        P(("gx", "gy"), None, None, None),
        P(),
        P(("gx", "gy"), None, None),
        P(),
        P(("gx", "gy"), None, None),
        P(("gx", "gy"), None, None),
    )
    return jax.shard_map(
        functools.partial(shards, mesh.shape["gx"], mesh.shape["gy"]),
        mesh=mesh,
        in_specs=placed,
        out_specs=P(("gx", "gy"), None, None, None),
        check_vma=False,
    )
```
